768 devices in a mesh: expert: 16 (over x, y_lo), replica: 48 (over y_hi, z, core).
Axes of the slice: x: 4, y: 8 (y_hi: 2, y_lo: 4; y = y_hi * 4 + y_lo), z: 12, core: 2. Of those that a mesh axis runs over, the one named last changes fastest.
Arguments:
- gradients: bfloat16 [48, 128, 48, 4096], P('replica', 'expert'), may hold values from -1792 to 1792
- master: float32 [128, 48, 4096], P('expert', 'replica'), may hold values from -400 to 400
- moment: float32 [128, 48, 4096], P('expert', 'replica'), may hold values from -4 to 4
- second: float32 [128, 48, 4096], P('expert', 'replica'), may hold values from 0.05 to 2
- loads: int32 [128], P('expert'), may hold values from 256 to 2047
- outlier_channels: int32 [128, 16], P('expert'), may hold values from 0 to 4095, as said below
- destination: int32 [128], P('expert'), may hold values from 0 to 127, as said below
Outputs:
- new_master: float32 [128, 48, 4096], P('expert', 'replica')
- new_moment: float32 [128, 48, 4096], P('expert', 'replica')
- new_second: float32 [128, 48, 4096], P('expert', 'replica')
- codes: bfloat16 [128, 48, 4096], P('expert', 'replica')
- scales: float32 [128, 48, 32], P('expert', 'replica')
- outlier_values: bfloat16 [128, 48, 16], P('expert', 'replica')
The draws below stay inside these ranges and needn't reach their ends.
Inputs may be any that keep to these rules, and one draw needn't show every extreme that they name: `outlier_channels`: 16 distinct channels for each expert. `destination`: a permutation of the slots; slot s lies on expert index s // 8; of the 8 experts of one expert index, at most 1 go to any one expert index (itself included), and exactly 1 to every index that gets any.
All inputs are finite; a program needn't handle non-finite values.
Results may differ from the reference program's by a relative error of at most 0.002.
Values sent between devices are 32-bit elements; how exact they have to be, the bound alone decides.
No kernel may reach another device: no remote copies, remote signals or barrier semaphores. Data moves between devices by JAX's collectives and lax.ppermute only.
A program may use at most 32 MiB of HBM per device.

```python
import math
import jax
import jax.numpy as jnp
from jax import lax

D = 4096
EXP_DEV = 8
GROUP = 128
OUTL = 16
EXPERTS = 128
WROWS = 48
CAP = 1
N_REPLICA = 48


def channel_sets(key):
    keys = jax.random.split(key, EXPERTS)
    picks = jax.vmap(lambda single: jax.random.permutation(single, D)[:OUTL])(keys)
    return picks.astype(jnp.int32)


def draw_outlier_channels(key, part):
    chosen = channel_sets(key)
    return chosen


def draw_master(key, part):
    chosen = channel_sets(key)
    key = jax.random.fold_in(key, 11)
    key_base, key_rows, key_cols = jax.random.split(key, 3)
    column = jnp.arange(D, dtype=jnp.int32)
    outlier_mask = jnp.any(chosen[:, :, None] == column[None, None, :], axis=1)
    base = jnp.clip(jax.random.normal(key_base, (EXPERTS, WROWS, D), jnp.float32), -4.0, 4.0)
    row_top = jnp.log(10.0)
    row_scale = jnp.exp(jax.random.uniform(key_rows, (EXPERTS, WROWS, 1), jnp.float32, 0.0, 1.0) * row_top)
    col_scale = jnp.exp(jax.random.uniform(key_cols, (EXPERTS, 1, D), jnp.float32, 0.0, jnp.log(10.0)))
    boost = jnp.where(outlier_mask[:, None, :], 8.0, 1.0)
    return (0.1 * base * row_scale * col_scale * boost).astype(jnp.float32)


def draw_destination(key, part):
    key = jax.random.fold_in(key, 5)
    count = EXPERTS // EXP_DEV
    width = EXP_DEV // CAP
    key_off, key_send, key_recv = jax.random.split(key, 3)
    offsets = jax.random.permutation(key_off, count)[:width].astype(jnp.int32)
    send_order = jax.vmap(lambda single: jax.random.permutation(single, EXP_DEV))(jax.random.split(key_send, count)).astype(jnp.int32)
    recv_order = jax.vmap(lambda single: jax.random.permutation(single, EXP_DEV))(jax.random.split(key_recv, count)).astype(jnp.int32)
    source = jnp.arange(count, dtype=jnp.int32)[:, None]
    which = send_order // CAP
    within = send_order % CAP
    target = (source + offsets[which]) % count
    local = recv_order[target, which * CAP + within]
    return (target * EXP_DEV + local).reshape(EXPERTS).astype(jnp.int32)


def place_ends(result, own_key, low, high):
    index_at = [jax.random.randint(jax.random.fold_in(own_key, axis), (), 0, length) for axis, length in enumerate(result.shape)]
    widest = result.shape.index(max(result.shape))
    beside = index_at[:widest] + [(index_at[widest] + 1) % result.shape[widest]] + index_at[widest + 1:]
    return result.at[tuple(index_at)].set(low).at[tuple(beside)].set(high)


def strengthened(values, stream_key, source, target, parts, factor):
    owner, partner = [(jnp.arange(values.shape[dim]) // (values.shape[dim] // parts)).reshape([-1 if axis == dim else 1 for axis in range(values.ndim)]) for dim in (source, target)]
    chosen = jax.random.permutation(stream_key, parts)[partner]
    strong = (owner == chosen) | (owner == (partner + parts // 2) % parts)
    return jnp.where(strong, factor * values, values)


def steps_of(stream_key, extent, cuts, smallest, top_value):
    loudness = 1.0
    for position, shards_of in cuts:
        draws = jax.random.uniform(jax.random.fold_in(jax.random.fold_in(stream_key, 6), position), (shards_of,), jnp.float32, smallest / len(cuts), top_value / len(cuts))
        loudness = loudness * jnp.repeat(jnp.exp(draws), extent[position] // shards_of).reshape((-1,) + (1,) * (len(extent) - 1 - position))
    return loudness


def centred(stream_key, dims, scale, reach, pieces=(), kind=jnp.bfloat16):
    factor_of = steps_of(stream_key, dims, pieces, -0.22, 0.18) if pieces else 1.0
    values = jax.random.normal(stream_key, dims, jnp.float32) * scale * factor_of
    return jnp.minimum(jnp.maximum(values, -reach), reach).astype(kind)


def heavy_noise(stream_key, extent, deviation, limit, cuts, heavy, kind=jnp.bfloat16):
    drawn = deviation * jax.random.normal(stream_key, extent, jnp.float32)
    if cuts:
        drawn = drawn * steps_of(stream_key, extent, cuts, -0.22, 0.18)
    return jnp.clip(strengthened(drawn, jax.random.fold_in(stream_key, 3), *heavy), -limit, limit).astype(kind)


def setup_inputs(seed: int = 0) -> dict:
    streams_of = jax.random.split(jax.random.key(seed), 8)
    gradients = heavy_noise(streams_of[0], (N_REPLICA, EXPERTS, WROWS, D), 128, 1792.0, ((0, 48), (1, 16)), (0, 2, 48, 3.25))
    master = draw_master(jax.random.fold_in(streams_of[7], 71), 0)
    moment = centred(streams_of[2], (EXPERTS, WROWS, D), 0.5, 4.0, ((0, 16), (1, 48)), jnp.float32)
    second = jnp.clip(jnp.exp(math.log(2.0) - 3.6888794 * jax.random.uniform(streams_of[3], (EXPERTS, WROWS, D), jnp.float32) ** steps_of(streams_of[3], (EXPERTS, WROWS, D), ((0, 16), (1, 48)), -0.2, 0.2)), 0.05, 2.0)
    loads = place_ends(jax.random.randint(streams_of[4], (EXPERTS,), 256, 2048), jax.random.fold_in(streams_of[4], 1), 256, 2047).astype(jnp.int32)
    outlier_channels = draw_outlier_channels(jax.random.fold_in(streams_of[7], 71), 0)
    destination = draw_destination(jax.random.fold_in(streams_of[7], 71), 0)
    return {"gradients": gradients, "master": master, "moment": moment, "second": second, "loads": loads, "outlier_channels": outlier_channels, "destination": destination}


beta_first = 0.9
beta_second = 0.95
bias_first = 1.0 / (1.0 - 0.9 ** 50)
bias_second = 1.0 / (1.0 - 0.95 ** 50)
epsilon_adam = 1e-08
learn_rate = 0.02
decay_rate = 0.1
quant_epsilon = 1e-06

def adam_update(grad_sum, master, moment, second, loads):
    grad = grad_sum / loads.astype(jnp.float32)[:, None, None]
    moment_next = beta_first * moment + (1.0 - beta_first) * grad
    second_next = beta_second * second + (1.0 - beta_second) * grad * grad
    update = moment_next * bias_first / (jnp.sqrt(second_next * bias_second) + epsilon_adam) + decay_rate * master
    return (master - learn_rate * update, moment_next, second_next)

def quantize(weights, channels):
    experts, rows, width = weights.shape
    column = jnp.arange(width, dtype=jnp.int32)
    outlier_mask = jnp.any(channels[:, :, None] == column[None, None, :], axis=1)
    masked = outlier_mask[:, None, :]
    magnitude = jnp.where(masked, 0.0, jnp.abs(weights)).reshape(experts, rows, width // GROUP, GROUP)
    scale = (lax.optimization_barrier(jnp.max(magnitude, axis=-1)) + quant_epsilon) / 7.0
    ratio = (weights.reshape(experts, rows, width // GROUP, GROUP) / scale[..., None]).reshape(experts, rows, width)
    codes = jnp.where(masked, 0.0, ratio).astype(jnp.bfloat16)
    picks = jnp.broadcast_to(channels[:, None, :], (experts, rows, channels.shape[1]))
    outliers = jnp.take_along_axis(weights, picks, axis=2).astype(jnp.bfloat16)
    return (codes, scale, outliers)

def reference(gradients, master, moment, second, loads, outlier_channels, destination):

    def accumulate(total, piece):
        return (total + piece.astype(jnp.float32), None)
    grad_sum, _ = lax.scan(accumulate, jnp.zeros(master.shape, jnp.float32), gradients)
    weights, moment_next, second_next = adam_update(grad_sum, master, moment, second, loads)
    codes, scale, outliers = quantize(weights, outlier_channels)

    def place(array):
        return jnp.zeros_like(array).at[destination].set(array)
    return (place(weights), place(moment_next), place(second_next), place(codes), place(scale), place(outliers))
```

```python
import jax
import jax.numpy as jnp
from jax import lax
from jax.experimental import pallas as pl
from jax.experimental.pallas import tpu as pltpu
from jax.sharding import Mesh
from jax.sharding import PartitionSpec as P

GROUP = 128
beta_first = 0.9
beta_second = 0.95
bias_first = 1.0 / (1.0 - 0.9**50)
bias_second = 1.0 / (1.0 - 0.95**50)
epsilon_adam = 1e-08
learn_rate = 0.02
decay_rate = 0.1
quant_epsilon = 1e-06

F32 = jnp.float32
VM = pltpu.VMEM
SM = pltpu.SMEM
Z = ("m", "s", "c")
E = 8
ROWS = 48
TILES = 32
CHUNK = 8
META = 8
STATE = 3 * TILES + META


def split_kernel(where_ref, g_ref, keep_ref, first_ref, rest_ref, rows_ref):
    core = where_ref[0]
    step = where_ref[1]
    for e in range(E):
        x = g_ref[0, e].astype(F32)
        for r in range(0, ROWS, 8):
            block = jnp.stack([x[r : r + 8, j * 128 : (j + 1) * 128] for j in range(CHUNK)])
            rows_ref[r : r + 8, e] = jnp.swapaxes(block, 0, 1)
    plus = lax.rem(step + 1, 3)
    minus = lax.rem(step + 2, 3)
    ahead = jnp.where(core == 0, plus, minus)
    behind = jnp.where(core == 0, minus, plus)
    other = 1 - core
    for i in range(8):
        keep_ref[0, i] = rows_ref[6 * i + 2 * ahead + core]
        keep_ref[1, i] = rows_ref[6 * i + 2 * behind + core]
        keep_ref[2, i] = rows_ref[6 * i + 2 * step + core]
        first_ref[i] = rows_ref[6 * i + 2 * behind + other]
        rest_ref[0, i] = rows_ref[6 * i + 2 * ahead + other]
        rest_ref[1, i] = rows_ref[6 * i + 2 * step + other]


def split(gradients, where):
    steps = TILES // CHUNK
    return pl.pallas_call(
        split_kernel,
        grid=(steps,),
        in_specs=[
            pl.BlockSpec(memory_space=SM),
            pl.BlockSpec((1, E, ROWS, CHUNK * 128), lambda j: (0, 0, 0, j)),
        ],
        out_specs=[
            pl.BlockSpec((3, 8, E, CHUNK, 128), lambda j: (0, 0, 0, j, 0)),
            pl.BlockSpec((8, E, CHUNK, 128), lambda j: (0, 0, j, 0)),
            pl.BlockSpec((2, 8, E, CHUNK, 128), lambda j: (0, 0, 0, j, 0)),
        ],
        out_shape=[
            jax.ShapeDtypeStruct((3, 8, E, TILES, 128), F32),
            jax.ShapeDtypeStruct((8, E, TILES, 128), F32),
            jax.ShapeDtypeStruct((2, 8, E, TILES, 128), F32),
        ],
        scratch_shapes=[VM((ROWS, E, CHUNK, 128), F32)],
        compiler_params=pltpu.CompilerParams(vmem_limit_bytes=32 << 20),
        name="split_rows",
    )(where, gradients)


def pack_state_kernel(dest_ref, master_ref, moment_ref, second_ref, meta_ref, out_ref):
    out_ref[...] = jnp.full(out_ref.shape, -1.0, F32)
    for e in range(E):
        slot = lax.shift_right_logical(dest_ref[e], 3)
        out_ref[slot, 0:TILES] = master_ref[e]
        out_ref[slot, TILES : 2 * TILES] = moment_ref[e]
        out_ref[slot, 2 * TILES : 3 * TILES] = second_ref[e]
        out_ref[slot, 3 * TILES : STATE] = jnp.broadcast_to(meta_ref[e : e + 1], (META, 128))


def pack_state(destination, master, moment, second, meta):
    return pl.pallas_call(
        pack_state_kernel,
        in_specs=[pl.BlockSpec(memory_space=SM)] + [pl.BlockSpec(memory_space=VM)] * 4,
        out_specs=pl.BlockSpec(memory_space=VM),
        out_shape=jax.ShapeDtypeStruct((16, STATE, 128), F32),
        name="pack_state",
    )(destination, master, moment, second, meta)


def pack_sum_kernel(dest_ref, parts_ref, out_ref):
    out_ref[...] = jnp.zeros(out_ref.shape, F32)
    for e in range(E):
        total = parts_ref[0, e]
        for i in range(1, 8):
            total = total + parts_ref[i, e]
        out_ref[lax.shift_right_logical(dest_ref[e], 3)] = total


def pack_sum(destination, parts):
    return pl.pallas_call(
        pack_sum_kernel,
        in_specs=[pl.BlockSpec(memory_space=SM), pl.BlockSpec(memory_space=VM)],
        out_specs=pl.BlockSpec(memory_space=VM),
        out_shape=jax.ShapeDtypeStruct((16, TILES, 128), F32),
        name="pack_sum",
    )(destination, parts)


def finish_kernel(
    src_ref, loads_ref, chan_ref, grad_ref, state_ref,
    master_ref, moment_ref, second_ref, codes_ref, scale_ref, outlier_ref,
):
    new = []
    for e in range(E):
        src = src_ref[e]
        grad = grad_ref[src] / loads_ref[e]
        master = state_ref[src, 0:TILES]
        moment = beta_first * state_ref[src, TILES : 2 * TILES] + (1.0 - beta_first) * grad
        second = (
            beta_second * state_ref[src, 2 * TILES : 3 * TILES]
            + (1.0 - beta_second) * grad * grad
        )
        update = (
            moment * bias_first / (jnp.sqrt(second * bias_second) + epsilon_adam)
            + decay_rate * master
        )
        weights = master - learn_rate * update
        master_ref[e] = weights
        moment_ref[e] = moment
        second_ref[e] = second
        new.append(weights)
    turned = jnp.swapaxes(jnp.stack(new), 0, 1)
    lane = lax.broadcasted_iota(jnp.int32, (E, 128), 1)
    channels = [jnp.broadcast_to(chan_ref[:, k : k + 1], (E, 128)) for k in range(16)]
    picked = [jnp.zeros((E, 128), F32) for _ in range(16)]
    scales = jnp.zeros((E, 128), F32)
    for g in range(TILES):
        row = turned[g]
        column = lane + g * 128
        masked = jnp.zeros((E, 128), jnp.bool_)
        for k in range(16):
            hit = column == channels[k]
            masked = jnp.logical_or(masked, hit)
            picked[k] = jnp.where(hit, row, picked[k])
        top = jnp.max(jnp.where(masked, 0.0, jnp.abs(row)), axis=1, keepdims=True)
        scale = (top + quant_epsilon) / 7.0
        codes_ref[:, g * 128 : (g + 1) * 128] = jnp.where(masked, 0.0, row / scale).astype(
            jnp.bfloat16
        )
        scales = jnp.where(lane == g, jnp.broadcast_to(scale, (E, 128)), scales)
    scale_ref[...] = scales[:, 0:TILES]
    outliers = jnp.zeros((E, 128), F32)
    for k in range(16):
        value = jnp.sum(picked[k], axis=1, keepdims=True)
        outliers = jnp.where(lane == k, jnp.broadcast_to(value, (E, 128)), outliers)
    outlier_ref[...] = outliers[:, 0:16].astype(jnp.bfloat16)


def finish(sources, loads, channels, grad, state):
    big = jax.ShapeDtypeStruct((E, TILES, 128), F32)
    return pl.pallas_call(
        finish_kernel,
        in_specs=[pl.BlockSpec(memory_space=SM)] * 2 + [pl.BlockSpec(memory_space=VM)] * 3,
        out_specs=[pl.BlockSpec(memory_space=VM)] * 6,
        out_shape=[
            big,
            big,
            big,
            jax.ShapeDtypeStruct((E, TILES * 128), jnp.bfloat16),
            jax.ShapeDtypeStruct((E, TILES), F32),
            jax.ShapeDtypeStruct((E, 16), jnp.bfloat16),
        ],
        name="adam_quantize",
    )(sources, loads, channels, grad, state)


def both_ways(array, turn):
    pairs = []
    for z in range(12):
        pairs.append((2 * z, 2 * ((z + turn) % 12)))
        pairs.append((2 * z + 1, 2 * ((z - turn) % 12) + 1))
    return lax.ppermute(array, Z, pairs)


def body(gradients, master, moment, second, loads, outlier_channels, destination):
    where = jnp.stack([lax.axis_index("c"), lax.axis_index("s")]).astype(jnp.int32)
    keep, first, rest = split(gradients, where)
    swap = [(0, 1), (1, 0)]
    first = keep[0] + lax.ppermute(first, "c", swap)
    rest = lax.ppermute(rest, "c", swap)
    from_first = both_ways(first, 1)
    from_second = both_ways(keep[1] + rest[0], -1)

    meta = jnp.concatenate(
        [jnp.bitwise_and(destination, 7)[:, None], loads[:, None], outlier_channels], axis=1
    ).astype(F32)
    meta = jnp.pad(meta, ((0, 0), (0, 128 - 18)))
    shape = (E, TILES, 128)
    state = pack_state(
        destination, master.reshape(shape), moment.reshape(shape), second.reshape(shape), meta
    )
    state = lax.all_to_all(state, ("x", "y"), split_axis=0, concat_axis=0, tiled=True)
    labels = state[:, 3 * TILES, :18]
    order = jnp.arange(E, dtype=F32)
    sources = jnp.argmax(labels[:, 0][None, :] == order[:, None], axis=1).astype(jnp.int32)
    chosen = jnp.sum(
        jnp.where((labels[:, 0][None, :] == order[:, None])[:, :, None], labels[None], 0.0), axis=1
    )
    loads_here = chosen[:, 1]
    channels_here = chosen[:, 2:18].astype(jnp.int32)

    total = keep[2] + rest[1] + from_first + from_second
    parts = lax.all_to_all(total, ("h", "m"), split_axis=0, concat_axis=0, tiled=True)
    grad = pack_sum(destination, parts)
    grad = lax.all_to_all(grad, ("x", "y"), split_axis=0, concat_axis=0, tiled=True)
    w, m, v, codes, scales, outliers = finish(sources, loads_here, channels_here, grad, state)
    full = (E, 1, TILES * 128)
    return (
        w.reshape(full),
        m.reshape(full),
        v.reshape(full),
        codes[:, None, :],
        scales[:, None, :],
        outliers[:, None, :],
    )


def solution(mesh):
    fine = Mesh(mesh.devices.reshape(4, 4, 2, 4, 3, 2), ("x", "y", "h", "m", "s", "c"))
    expert = ("x", "y")
    replica = ("h", "m", "s", "c")
    state = P(expert, replica, None)
    in_specs = (
        P(replica, expert, None, None),
        state,
        state,
        state,
        P(expert),
        P(expert, None),
        P(expert),
    )
    return jax.shard_map(body, mesh=fine, in_specs=in_specs, out_specs=(state,) * 6, check_vma=False)
```

```python
import jax
import jax.numpy as jnp
from jax import lax
from jax.experimental import pallas as pl
from jax.experimental.pallas import tpu as pltpu
from jax.sharding import Mesh
from jax.sharding import PartitionSpec as P

GROUP = 128
beta_first = 0.9
beta_second = 0.95
bias_first = 1.0 / (1.0 - 0.9**50)
bias_second = 1.0 / (1.0 - 0.95**50)
epsilon_adam = 1e-08
learn_rate = 0.02
decay_rate = 0.1
quant_epsilon = 1e-06

F32 = jnp.float32
VM = pltpu.VMEM
SM = pltpu.SMEM
Z = ("m", "s", "c")
E = 8
ROWS = 48
TILES = 32
CHUNK = 8
META = 8
STATE = 3 * TILES + META


def split_kernel(
    where_ref, g_ref, ahead_ref, behind_ref, mine_ref, first_ref, rest_ref, rows_ref
):
    core = where_ref[0]
    step = where_ref[1]
    for e in range(E):
        x = g_ref[0, e].astype(F32)
        for r in range(0, ROWS, 8):
            block = jnp.stack([x[r : r + 8, j * 128 : (j + 1) * 128] for j in range(CHUNK)])
            rows_ref[r : r + 8, e] = jnp.swapaxes(block, 0, 1)
    plus = lax.rem(step + 1, 3)
    minus = lax.rem(step + 2, 3)
    ahead = jnp.where(core == 0, plus, minus)
    behind = jnp.where(core == 0, minus, plus)
    other = 1 - core
    for i in range(8):
        ahead_ref[i] = rows_ref[6 * i + 2 * ahead + core]
        behind_ref[i] = rows_ref[6 * i + 2 * behind + core]
        mine_ref[i] = rows_ref[6 * i + 2 * step + core]
        first_ref[i] = rows_ref[6 * i + 2 * behind + other]
        rest_ref[0, i] = rows_ref[6 * i + 2 * ahead + other]
        rest_ref[1, i] = rows_ref[6 * i + 2 * step + other]


def split(gradients, where):
    steps = TILES // CHUNK
    return pl.pallas_call(
        split_kernel,
        grid=(steps,),
        in_specs=[
            pl.BlockSpec(memory_space=SM),
            pl.BlockSpec((1, E, ROWS, CHUNK * 128), lambda j: (0, 0, 0, j)),
        ],
        out_specs=[
            pl.BlockSpec((8, E, CHUNK, 128), lambda j: (0, 0, j, 0)),
            pl.BlockSpec((8, E, CHUNK, 128), lambda j: (0, 0, j, 0)),
            pl.BlockSpec((8, E, CHUNK, 128), lambda j: (0, 0, j, 0)),
            pl.BlockSpec((8, E, CHUNK, 128), lambda j: (0, 0, j, 0)),
            pl.BlockSpec((2, 8, E, CHUNK, 128), lambda j: (0, 0, 0, j, 0)),
        ],
        out_shape=[
            jax.ShapeDtypeStruct((8, E, TILES, 128), F32),
            jax.ShapeDtypeStruct((8, E, TILES, 128), F32),
            jax.ShapeDtypeStruct((8, E, TILES, 128), F32),
            jax.ShapeDtypeStruct((8, E, TILES, 128), F32),
            jax.ShapeDtypeStruct((2, 8, E, TILES, 128), F32),
        ],
        scratch_shapes=[VM((ROWS, E, CHUNK, 128), F32)],
        compiler_params=pltpu.CompilerParams(vmem_limit_bytes=12 << 20),
        name="split_rows",
    )(where, gradients)


def pack_state_kernel(dest_ref, master_ref, moment_ref, second_ref, meta_ref, out_ref):
    out_ref[...] = jnp.full(out_ref.shape, -1.0, F32)
    for e in range(E):
        slot = lax.shift_right_logical(dest_ref[e], 3)
        out_ref[slot, 0:TILES] = master_ref[e]
        out_ref[slot, TILES : 2 * TILES] = moment_ref[e]
        out_ref[slot, 2 * TILES : 3 * TILES] = second_ref[e]
        out_ref[slot, 3 * TILES : STATE] = jnp.broadcast_to(meta_ref[e : e + 1], (META, 128))


def pack_state(destination, master, moment, second, meta):
    return pl.pallas_call(
        pack_state_kernel,
        in_specs=[pl.BlockSpec(memory_space=SM)] + [pl.BlockSpec(memory_space=VM)] * 4,
        out_specs=pl.BlockSpec(memory_space=VM),
        out_shape=jax.ShapeDtypeStruct((16, STATE, 128), F32),
        compiler_params=pltpu.CompilerParams(vmem_limit_bytes=8 << 20),
        name="pack_state",
    )(destination, master, moment, second, meta)


def pack_sum_kernel(dest_ref, parts_ref, out_ref):
    out_ref[...] = jnp.zeros(out_ref.shape, F32)
    for e in range(E):
        total = parts_ref[0, e]
        for i in range(1, 8):
            total = total + parts_ref[i, e]
        out_ref[lax.shift_right_logical(dest_ref[e], 3)] = total


def pack_sum(destination, parts):
    return pl.pallas_call(
        pack_sum_kernel,
        in_specs=[pl.BlockSpec(memory_space=SM), pl.BlockSpec(memory_space=VM)],
        out_specs=pl.BlockSpec(memory_space=VM),
        out_shape=jax.ShapeDtypeStruct((16, TILES, 128), F32),
        compiler_params=pltpu.CompilerParams(vmem_limit_bytes=8 << 20),
        name="pack_sum",
    )(destination, parts)


def finish_kernel(
    src_ref, loads_ref, chan_ref, grad_ref, state_ref,
    master_ref, moment_ref, second_ref, codes_ref, scale_ref, outlier_ref,
):
    new = []
    for e in range(E):
        src = src_ref[e]
        grad = grad_ref[src] / loads_ref[e]
        master = state_ref[src, 0:TILES]
        moment = beta_first * state_ref[src, TILES : 2 * TILES] + (1.0 - beta_first) * grad
        second = (
            beta_second * state_ref[src, 2 * TILES : 3 * TILES]
            + (1.0 - beta_second) * grad * grad
        )
        update = (
            moment * bias_first / (jnp.sqrt(second * bias_second) + epsilon_adam)
            + decay_rate * master
        )
        weights = master - learn_rate * update
        master_ref[e] = weights
        moment_ref[e] = moment
        second_ref[e] = second
        new.append(weights)
    turned = jnp.swapaxes(jnp.stack(new), 0, 1)
    lane = lax.broadcasted_iota(jnp.int32, (E, 128), 1)
    channels = [jnp.broadcast_to(chan_ref[:, k : k + 1], (E, 128)) for k in range(16)]
    picked = [jnp.zeros((E, 128), F32) for _ in range(16)]
    scales = jnp.zeros((E, 128), F32)
    for g in range(TILES):
        row = turned[g]
        column = lane + g * 128
        masked = jnp.zeros((E, 128), jnp.bool_)
        for k in range(16):
            hit = column == channels[k]
            masked = jnp.logical_or(masked, hit)
            picked[k] = jnp.where(hit, row, picked[k])
        top = jnp.max(jnp.where(masked, 0.0, jnp.abs(row)), axis=1, keepdims=True)
        scale = (top + quant_epsilon) / 7.0
        codes_ref[:, g * 128 : (g + 1) * 128] = jnp.where(masked, 0.0, row / scale).astype(
            jnp.bfloat16
        )
        scales = jnp.where(lane == g, jnp.broadcast_to(scale, (E, 128)), scales)
    scale_ref[...] = scales[:, 0:TILES]
    outliers = jnp.zeros((E, 128), F32)
    for k in range(16):
        value = jnp.sum(picked[k], axis=1, keepdims=True)
        outliers = jnp.where(lane == k, jnp.broadcast_to(value, (E, 128)), outliers)
    outlier_ref[...] = outliers[:, 0:16].astype(jnp.bfloat16)


def finish(sources, loads, channels, grad, state):
    big = jax.ShapeDtypeStruct((E, TILES, 128), F32)
    return pl.pallas_call(
        finish_kernel,
        in_specs=[pl.BlockSpec(memory_space=SM)] * 2 + [pl.BlockSpec(memory_space=VM)] * 3,
        out_specs=[pl.BlockSpec(memory_space=VM)] * 6,
        out_shape=[
            big,
            big,
            big,
            jax.ShapeDtypeStruct((E, TILES * 128), jnp.bfloat16),
            jax.ShapeDtypeStruct((E, TILES), F32),
            jax.ShapeDtypeStruct((E, 16), jnp.bfloat16),
        ],
        compiler_params=pltpu.CompilerParams(vmem_limit_bytes=8 << 20),
        name="adam_quantize",
    )(sources, loads, channels, grad, state)


def both_ways(array, turn):
    pairs = []
    for z in range(12):
        pairs.append((2 * z, 2 * ((z + turn) % 12)))
        pairs.append((2 * z + 1, 2 * ((z - turn) % 12) + 1))
    return lax.ppermute(array, Z, pairs)


def body(gradients, master, moment, second, loads, outlier_channels, destination):
    where = jnp.stack([lax.axis_index("c"), lax.axis_index("s")]).astype(jnp.int32)
    ahead, behind, mine, first, rest = split(gradients, where)
    swap = [(0, 1), (1, 0)]
    first = ahead + lax.ppermute(first, "c", swap)
    rest = lax.ppermute(rest, "c", swap)
    from_first = both_ways(first, 1)
    from_second = both_ways(behind + rest[0], -1)

    meta = jnp.concatenate(
        [jnp.bitwise_and(destination, 7)[:, None], loads[:, None], outlier_channels], axis=1
    ).astype(F32)
    meta = jnp.pad(meta, ((0, 0), (0, 128 - 18)))
    shape = (E, TILES, 128)
    state = pack_state(
        destination, master.reshape(shape), moment.reshape(shape), second.reshape(shape), meta
    )
    state = lax.all_to_all(state, ("x", "y"), split_axis=0, concat_axis=0, tiled=True)
    labels = state[:, 3 * TILES, :18]
    order = jnp.arange(E, dtype=F32)
    sources = jnp.argmax(labels[:, 0][None, :] == order[:, None], axis=1).astype(jnp.int32)
    chosen = jnp.sum(
        jnp.where((labels[:, 0][None, :] == order[:, None])[:, :, None], labels[None], 0.0), axis=1
    )
    loads_here = chosen[:, 1]
    channels_here = chosen[:, 2:18].astype(jnp.int32)

    partial = lax.optimization_barrier(mine + rest[1] + from_first)
    total = partial + from_second
    parts = lax.all_to_all(total, ("h", "m"), split_axis=0, concat_axis=0, tiled=True)
    grad = pack_sum(destination, parts)
    grad = lax.all_to_all(grad, ("x", "y"), split_axis=0, concat_axis=0, tiled=True)
    w, m, v, codes, scales, outliers = finish(sources, loads_here, channels_here, grad, state)
    full = (E, 1, TILES * 128)
    return (
        w.reshape(full),
        m.reshape(full),
        v.reshape(full),
        codes[:, None, :],
        scales[:, None, :],
        outliers[:, None, :],
    )


def solution(mesh):
    fine = Mesh(mesh.devices.reshape(4, 4, 2, 4, 3, 2), ("x", "y", "h", "m", "s", "c"))
    expert = ("x", "y")
    replica = ("h", "m", "s", "c")
    state = P(expert, replica, None)
    in_specs = (
        P(replica, expert, None, None),
        state,
        state,
        state,
        P(expert),
        P(expert, None),
        P(expert),
    )
    return jax.shard_map(body, mesh=fine, in_specs=in_specs, out_specs=(state,) * 6, check_vma=False)
```

```python
import jax
import jax.numpy as jnp
from jax import lax
from jax.experimental import pallas as pl
from jax.experimental.pallas import tpu as pltpu
from jax.sharding import Mesh
from jax.sharding import PartitionSpec as P

GROUP = 128
beta_first = 0.9
beta_second = 0.95
bias_first = 1.0 / (1.0 - 0.9**50)
bias_second = 1.0 / (1.0 - 0.95**50)
epsilon_adam = 1e-08
learn_rate = 0.02
decay_rate = 0.1
quant_epsilon = 1e-06

F32 = jnp.float32
VM = pltpu.VMEM
SM = pltpu.SMEM
Z = ("m", "s", "c")
E = 8
ROWS = 48
TILES = 32
CHUNK = 8
META = 8
STATE = 3 * TILES + META


def split_kernel(
    where_ref, g_ref, ahead_ref, behind_ref, mine_ref, first_ref, next_ref, last_ref, rows_ref
):
    core = where_ref[0]
    step = where_ref[1]
    for e in range(E):
        x = g_ref[0, e].astype(F32)
        for r in range(0, ROWS, 8):
            block = jnp.stack([x[r : r + 8, j * 128 : (j + 1) * 128] for j in range(CHUNK)])
            rows_ref[r : r + 8, e] = jnp.swapaxes(block, 0, 1)
    plus = lax.rem(step + 1, 3)
    minus = lax.rem(step + 2, 3)
    ahead = jnp.where(core == 0, plus, minus)
    behind = jnp.where(core == 0, minus, plus)
    other = 1 - core
    for i in range(8):
        ahead_ref[i] = rows_ref[6 * i + 2 * ahead + core]
        behind_ref[i] = rows_ref[6 * i + 2 * behind + core]
        mine_ref[i] = rows_ref[6 * i + 2 * step + core]
        first_ref[i] = rows_ref[6 * i + 2 * behind + other]
        next_ref[i] = rows_ref[6 * i + 2 * ahead + other]
        last_ref[i] = rows_ref[6 * i + 2 * step + other]


def split(gradients, where):
    steps = TILES // CHUNK
    return pl.pallas_call(
        split_kernel,
        grid=(steps,),
        in_specs=[
            pl.BlockSpec(memory_space=SM),
            pl.BlockSpec((1, E, ROWS, CHUNK * 128), lambda j: (0, 0, 0, j)),
        ],
        out_specs=[pl.BlockSpec((8, E, CHUNK, 128), lambda j: (0, 0, j, 0))] * 6,
        out_shape=[jax.ShapeDtypeStruct((8, E, TILES, 128), F32)] * 6,
        scratch_shapes=[VM((ROWS, E, CHUNK, 128), F32)],
        compiler_params=pltpu.CompilerParams(vmem_limit_bytes=12 << 20),
        name="split_rows",
    )(where, gradients)


def pack_state_kernel(dest_ref, master_ref, moment_ref, second_ref, meta_ref, out_ref):
    out_ref[...] = jnp.full(out_ref.shape, -1.0, F32)
    for e in range(E):
        slot = lax.shift_right_logical(dest_ref[e], 3)
        out_ref[slot, 0:TILES] = master_ref[e]
        out_ref[slot, TILES : 2 * TILES] = moment_ref[e]
        out_ref[slot, 2 * TILES : 3 * TILES] = second_ref[e]
        out_ref[slot, 3 * TILES : STATE] = jnp.broadcast_to(meta_ref[e : e + 1], (META, 128))


def pack_state(destination, master, moment, second, meta):
    return pl.pallas_call(
        pack_state_kernel,
        in_specs=[pl.BlockSpec(memory_space=SM)] + [pl.BlockSpec(memory_space=VM)] * 4,
        out_specs=pl.BlockSpec(memory_space=VM),
        out_shape=jax.ShapeDtypeStruct((16, STATE, 128), F32),
        compiler_params=pltpu.CompilerParams(vmem_limit_bytes=8 << 20),
        name="pack_state",
    )(destination, master, moment, second, meta)


def pack_sum_kernel(dest_ref, parts_ref, out_ref):
    out_ref[...] = jnp.zeros(out_ref.shape, F32)
    for e in range(E):
        total = parts_ref[0, e]
        for i in range(1, 8):
            total = total + parts_ref[i, e]
        out_ref[lax.shift_right_logical(dest_ref[e], 3)] = total


def pack_sum(destination, parts):
    return pl.pallas_call(
        pack_sum_kernel,
        in_specs=[pl.BlockSpec(memory_space=SM), pl.BlockSpec(memory_space=VM)],
        out_specs=pl.BlockSpec(memory_space=VM),
        out_shape=jax.ShapeDtypeStruct((16, TILES, 128), F32),
        compiler_params=pltpu.CompilerParams(vmem_limit_bytes=8 << 20),
        name="pack_sum",
    )(destination, parts)


def finish_kernel(
    src_ref, loads_ref, chan_ref, grad_ref, state_ref,
    master_ref, moment_ref, second_ref, codes_ref, scale_ref, outlier_ref,
):
    new = []
    for e in range(E):
        src = src_ref[e]
        grad = grad_ref[src] / loads_ref[e]
        master = state_ref[src, 0:TILES]
        moment = beta_first * state_ref[src, TILES : 2 * TILES] + (1.0 - beta_first) * grad
        second = (
            beta_second * state_ref[src, 2 * TILES : 3 * TILES]
            + (1.0 - beta_second) * grad * grad
        )
        update = (
            moment * bias_first / (jnp.sqrt(second * bias_second) + epsilon_adam)
            + decay_rate * master
        )
        weights = master - learn_rate * update
        master_ref[e] = weights
        moment_ref[e] = moment
        second_ref[e] = second
        new.append(weights)
    turned = jnp.swapaxes(jnp.stack(new), 0, 1)
    lane = lax.broadcasted_iota(jnp.int32, (E, 128), 1)
    channels = [jnp.broadcast_to(chan_ref[:, k : k + 1], (E, 128)) for k in range(16)]
    picked = [jnp.zeros((E, 128), F32) for _ in range(16)]
    scales = jnp.zeros((E, 128), F32)
    for g in range(TILES):
        row = turned[g]
        column = lane + g * 128
        masked = jnp.zeros((E, 128), jnp.bool_)
        for k in range(16):
            hit = column == channels[k]
            masked = jnp.logical_or(masked, hit)
            picked[k] = jnp.where(hit, row, picked[k])
        top = jnp.max(jnp.where(masked, 0.0, jnp.abs(row)), axis=1, keepdims=True)
        scale = (top + quant_epsilon) / 7.0
        codes_ref[:, g * 128 : (g + 1) * 128] = jnp.where(masked, 0.0, row / scale).astype(
            jnp.bfloat16
        )
        scales = jnp.where(lane == g, jnp.broadcast_to(scale, (E, 128)), scales)
    scale_ref[...] = scales[:, 0:TILES]
    outliers = jnp.zeros((E, 128), F32)
    for k in range(16):
        value = jnp.sum(picked[k], axis=1, keepdims=True)
        outliers = jnp.where(lane == k, jnp.broadcast_to(value, (E, 128)), outliers)
    outlier_ref[...] = outliers[:, 0:16].astype(jnp.bfloat16)


def finish(sources, loads, channels, grad, state):
    big = jax.ShapeDtypeStruct((E, TILES, 128), F32)
    return pl.pallas_call(
        finish_kernel,
        in_specs=[pl.BlockSpec(memory_space=SM)] * 2 + [pl.BlockSpec(memory_space=VM)] * 3,
        out_specs=[pl.BlockSpec(memory_space=VM)] * 6,
        out_shape=[
            big,
            big,
            big,
            jax.ShapeDtypeStruct((E, TILES * 128), jnp.bfloat16),
            jax.ShapeDtypeStruct((E, TILES), F32),
            jax.ShapeDtypeStruct((E, 16), jnp.bfloat16),
        ],
        compiler_params=pltpu.CompilerParams(vmem_limit_bytes=8 << 20),
        name="adam_quantize",
    )(sources, loads, channels, grad, state)


def both_ways(array, turn):
    pairs = []
    for z in range(12):
        pairs.append((2 * z, 2 * ((z + turn) % 12)))
        pairs.append((2 * z + 1, 2 * ((z - turn) % 12) + 1))
    return lax.ppermute(array, Z, pairs)


def body(gradients, master, moment, second, loads, outlier_channels, destination):
    where = jnp.stack([lax.axis_index("c"), lax.axis_index("s")]).astype(jnp.int32)
    ahead, behind, mine, first, follow, last = split(gradients, where)
    swap = [(0, 1), (1, 0)]
    first = ahead + lax.ppermute(first, "c", swap)
    follow = lax.ppermute(follow, "c", swap)
    last = lax.ppermute(last, "c", swap)
    from_first = both_ways(first, 1)
    outgoing, from_first = lax.optimization_barrier((behind + follow, from_first))
    from_second = both_ways(outgoing, -1)

    meta = jnp.concatenate(
        [jnp.bitwise_and(destination, 7)[:, None], loads[:, None], outlier_channels], axis=1
    ).astype(F32)
    meta = jnp.pad(meta, ((0, 0), (0, 128 - 18)))
    shape = (E, TILES, 128)
    state = pack_state(
        destination, master.reshape(shape), moment.reshape(shape), second.reshape(shape), meta
    )
    state = lax.all_to_all(state, ("x", "y"), split_axis=0, concat_axis=0, tiled=True)
    labels = state[:, 3 * TILES, :18]
    order = jnp.arange(E, dtype=F32)
    sources = jnp.argmax(labels[:, 0][None, :] == order[:, None], axis=1).astype(jnp.int32)
    chosen = jnp.sum(
        jnp.where((labels[:, 0][None, :] == order[:, None])[:, :, None], labels[None], 0.0), axis=1
    )
    loads_here = chosen[:, 1]
    channels_here = chosen[:, 2:18].astype(jnp.int32)

    partial = lax.optimization_barrier(mine + last + from_first)
    total = partial + from_second
    parts = lax.all_to_all(total, ("h", "m"), split_axis=0, concat_axis=0, tiled=True)
    grad = pack_sum(destination, parts)
    grad = lax.all_to_all(grad, ("x", "y"), split_axis=0, concat_axis=0, tiled=True)
    w, m, v, codes, scales, outliers = finish(sources, loads_here, channels_here, grad, state)
    full = (E, 1, TILES * 128)
    return (
        w.reshape(full),
        m.reshape(full),
        v.reshape(full),
        codes[:, None, :],
        scales[:, None, :],
        outliers[:, None, :],
    )


def solution(mesh):
    fine = Mesh(mesh.devices.reshape(4, 4, 2, 4, 3, 2), ("x", "y", "h", "m", "s", "c"))
    expert = ("x", "y")
    replica = ("h", "m", "s", "c")
    state = P(expert, replica, None)
    in_specs = (
        P(replica, expert, None, None),
        state,
        state,
        state,
        P(expert),
        P(expert, None),
        P(expert),
    )
    return jax.shard_map(body, mesh=fine, in_specs=in_specs, out_specs=(state,) * 6, check_vma=False)
```

```python
import jax
import jax.numpy as jnp
from jax import lax
from jax.experimental import pallas as pl
from jax.experimental.pallas import tpu as pltpu
from jax.sharding import Mesh
from jax.sharding import PartitionSpec as P

GROUP = 128
beta_first = 0.9
beta_second = 0.95
bias_first = 1.0 / (1.0 - 0.9**50)
bias_second = 1.0 / (1.0 - 0.95**50)
epsilon_adam = 1e-08
learn_rate = 0.02
decay_rate = 0.1
quant_epsilon = 1e-06

F32 = jnp.float32
VM = pltpu.VMEM
SM = pltpu.SMEM
Z = ("m", "s", "c")
E = 8
ROWS = 48
TILES = 32
CHUNK = 8
META = 8
STATE = 3 * TILES + META


def split_kernel(
    where_ref, g_ref, ahead_ref, behind_ref, mine_ref, first_ref, next_ref, last_ref, rows_ref
):
    core = where_ref[0]
    step = where_ref[1]
    for e in range(E):
        x = g_ref[0, e].astype(F32)
        for r in range(0, ROWS, 8):
            block = jnp.stack([x[r : r + 8, j * 128 : (j + 1) * 128] for j in range(CHUNK)])
            rows_ref[r : r + 8, e] = jnp.swapaxes(block, 0, 1)
    plus = lax.rem(step + 1, 3)
    minus = lax.rem(step + 2, 3)
    ahead = jnp.where(core == 0, plus, minus)
    behind = jnp.where(core == 0, minus, plus)
    other = 1 - core
    for i in range(8):
        row = 6 * (4 * (i % 2) + i // 2)
        ahead_ref[i] = rows_ref[row + 2 * ahead + core]
        behind_ref[i] = rows_ref[row + 2 * behind + core]
        mine_ref[i] = rows_ref[row + 2 * step + core]
        first_ref[i] = rows_ref[row + 2 * behind + other]
        next_ref[i] = rows_ref[row + 2 * ahead + other]
        last_ref[i] = rows_ref[row + 2 * step + other]


def split(gradients, where):
    steps = TILES // CHUNK
    return pl.pallas_call(
        split_kernel,
        grid=(steps,),
        in_specs=[
            pl.BlockSpec(memory_space=SM),
            pl.BlockSpec((1, E, ROWS, CHUNK * 128), lambda j: (0, 0, 0, j)),
        ],
        out_specs=[pl.BlockSpec((8, E, CHUNK, 128), lambda j: (0, 0, j, 0))] * 6,
        out_shape=[jax.ShapeDtypeStruct((8, E, TILES, 128), F32)] * 6,
        scratch_shapes=[VM((ROWS, E, CHUNK, 128), F32)],
        compiler_params=pltpu.CompilerParams(vmem_limit_bytes=12 << 20),
        name="split_rows",
    )(where, gradients)


def pack_state_kernel(dest_ref, master_ref, moment_ref, second_ref, meta_ref, out_ref):
    out_ref[...] = jnp.full(out_ref.shape, -1.0, F32)
    for e in range(E):
        slot = lax.shift_right_logical(dest_ref[e], 3)
        out_ref[slot, 0:TILES] = master_ref[e]
        out_ref[slot, TILES : 2 * TILES] = moment_ref[e]
        out_ref[slot, 2 * TILES : 3 * TILES] = second_ref[e]
        out_ref[slot, 3 * TILES : STATE] = jnp.broadcast_to(meta_ref[e : e + 1], (META, 128))


def pack_state(destination, master, moment, second, meta):
    return pl.pallas_call(
        pack_state_kernel,
        in_specs=[pl.BlockSpec(memory_space=SM)] + [pl.BlockSpec(memory_space=VM)] * 4,
        out_specs=pl.BlockSpec(memory_space=VM),
        out_shape=jax.ShapeDtypeStruct((16, STATE, 128), F32),
        compiler_params=pltpu.CompilerParams(vmem_limit_bytes=8 << 20),
        name="pack_state",
    )(destination, master, moment, second, meta)


def pack_sum_kernel(dest_ref, parts_ref, out_ref):
    out_ref[...] = jnp.zeros(out_ref.shape, F32)
    for e in range(E):
        total = parts_ref[0, e]
        for i in range(1, 8):
            total = total + parts_ref[i, e]
        out_ref[lax.shift_right_logical(dest_ref[e], 3)] = total


def pack_sum(destination, parts):
    return pl.pallas_call(
        pack_sum_kernel,
        in_specs=[pl.BlockSpec(memory_space=SM), pl.BlockSpec(memory_space=VM)],
        out_specs=pl.BlockSpec(memory_space=VM),
        out_shape=jax.ShapeDtypeStruct((16, TILES, 128), F32),
        compiler_params=pltpu.CompilerParams(vmem_limit_bytes=8 << 20),
        name="pack_sum",
    )(destination, parts)


def finish_kernel(
    src_ref, loads_ref, chan_ref, grad_ref, state_ref,
    master_ref, moment_ref, second_ref, codes_ref, scale_ref, outlier_ref,
):
    new = []
    for e in range(E):
        src = src_ref[e]
        grad = grad_ref[src] / loads_ref[e]
        master = state_ref[src, 0:TILES]
        moment = beta_first * state_ref[src, TILES : 2 * TILES] + (1.0 - beta_first) * grad
        second = (
            beta_second * state_ref[src, 2 * TILES : 3 * TILES]
            + (1.0 - beta_second) * grad * grad
        )
        update = (
            moment * bias_first / (jnp.sqrt(second * bias_second) + epsilon_adam)
            + decay_rate * master
        )
        weights = master - learn_rate * update
        master_ref[e] = weights
        moment_ref[e] = moment
        second_ref[e] = second
        new.append(weights)
    turned = jnp.swapaxes(jnp.stack(new), 0, 1)
    lane = lax.broadcasted_iota(jnp.int32, (E, 128), 1)
    channels = [jnp.broadcast_to(chan_ref[:, k : k + 1], (E, 128)) for k in range(16)]
    picked = [jnp.zeros((E, 128), F32) for _ in range(16)]
    scales = jnp.zeros((E, 128), F32)
    for g in range(TILES):
        row = turned[g]
        column = lane + g * 128
        masked = jnp.zeros((E, 128), jnp.bool_)
        for k in range(16):
            hit = column == channels[k]
            masked = jnp.logical_or(masked, hit)
            picked[k] = jnp.where(hit, row, picked[k])
        top = jnp.max(jnp.where(masked, 0.0, jnp.abs(row)), axis=1, keepdims=True)
        scale = (top + quant_epsilon) / 7.0
        codes_ref[:, g * 128 : (g + 1) * 128] = jnp.where(masked, 0.0, row / scale).astype(
            jnp.bfloat16
        )
        scales = jnp.where(lane == g, jnp.broadcast_to(scale, (E, 128)), scales)
    scale_ref[...] = scales[:, 0:TILES]
    outliers = jnp.zeros((E, 128), F32)
    for k in range(16):
        value = jnp.sum(picked[k], axis=1, keepdims=True)
        outliers = jnp.where(lane == k, jnp.broadcast_to(value, (E, 128)), outliers)
    outlier_ref[...] = outliers[:, 0:16].astype(jnp.bfloat16)


def finish(sources, loads, channels, grad, state):
    big = jax.ShapeDtypeStruct((E, TILES, 128), F32)
    return pl.pallas_call(
        finish_kernel,
        in_specs=[pl.BlockSpec(memory_space=SM)] * 2 + [pl.BlockSpec(memory_space=VM)] * 3,
        out_specs=[pl.BlockSpec(memory_space=VM)] * 6,
        out_shape=[
            big,
            big,
            big,
            jax.ShapeDtypeStruct((E, TILES * 128), jnp.bfloat16),
            jax.ShapeDtypeStruct((E, TILES), F32),
            jax.ShapeDtypeStruct((E, 16), jnp.bfloat16),
        ],
        compiler_params=pltpu.CompilerParams(vmem_limit_bytes=8 << 20),
        name="adam_quantize",
    )(sources, loads, channels, grad, state)


def both_ways(array, turn):
    pairs = []
    for z in range(12):
        pairs.append((2 * z, 2 * ((z + turn) % 12)))
        pairs.append((2 * z + 1, 2 * ((z - turn) % 12) + 1))
    return lax.ppermute(array, Z, pairs)


def body(gradients, master, moment, second, loads, outlier_channels, destination):
    where = jnp.stack([lax.axis_index("c"), lax.axis_index("s")]).astype(jnp.int32)
    ahead, behind, mine, first, follow, last = split(gradients, where)
    swap = [(0, 1), (1, 0)]
    first = ahead + lax.ppermute(first, "c", swap)
    follow = lax.ppermute(follow, "c", swap)
    last = lax.ppermute(last, "c", swap)
    from_first = both_ways(first, 1)
    outgoing, from_first = lax.optimization_barrier((behind + follow, from_first))
    from_second = both_ways(outgoing, -1)

    meta = jnp.concatenate(
        [jnp.bitwise_and(destination, 7)[:, None], loads[:, None], outlier_channels], axis=1
    ).astype(F32)
    meta = jnp.pad(meta, ((0, 0), (0, 128 - 18)))
    shape = (E, TILES, 128)
    state = pack_state(
        destination, master.reshape(shape), moment.reshape(shape), second.reshape(shape), meta
    )
    state = lax.all_to_all(state, ("x", "y"), split_axis=0, concat_axis=0, tiled=True)
    labels = state[:, 3 * TILES, :18]
    order = jnp.arange(E, dtype=F32)
    sources = jnp.argmax(labels[:, 0][None, :] == order[:, None], axis=1).astype(jnp.int32)
    chosen = jnp.sum(
        jnp.where((labels[:, 0][None, :] == order[:, None])[:, :, None], labels[None], 0.0), axis=1
    )
    loads_here = chosen[:, 1]
    channels_here = chosen[:, 2:18].astype(jnp.int32)

    partial = lax.optimization_barrier(mine + last + from_first)
    total = partial + from_second
    parts = lax.all_to_all(total, ("m", "h"), split_axis=0, concat_axis=0, tiled=True)
    grad = pack_sum(destination, parts)
    grad = lax.all_to_all(grad, ("x", "y"), split_axis=0, concat_axis=0, tiled=True)
    w, m, v, codes, scales, outliers = finish(sources, loads_here, channels_here, grad, state)
    full = (E, 1, TILES * 128)
    return (
        w.reshape(full),
        m.reshape(full),
        v.reshape(full),
        codes[:, None, :],
        scales[:, None, :],
        outliers[:, None, :],
    )


def solution(mesh):
    fine = Mesh(mesh.devices.reshape(4, 4, 2, 4, 3, 2), ("x", "y", "h", "m", "s", "c"))
    expert = ("x", "y")
    replica = ("h", "m", "s", "c")
    state = P(expert, replica, None)
    in_specs = (
        P(replica, expert, None, None),
        state,
        state,
        state,
        P(expert),
        P(expert, None),
        P(expert),
    )
    return jax.shard_map(body, mesh=fine, in_specs=in_specs, out_specs=(state,) * 6, check_vma=False)
```
